32 devices in a mesh: groups: 2 (over y), tp: 4 (over x, core), pool: 4 (over z).
Axes of the slice: x: 2, y: 2, z: 4, core: 2. Of those that a mesh axis runs over, the one named last changes fastest.
Arguments:
- frames: bfloat16 [4096, 5120], P(('groups', 'pool'), 'tp'), parts along dimension 0, may hold values from -6 to 6
- norm_gain: bfloat16 [5120], P('tp'), may hold values from 0.099609375 to 1.8984375
- kv_weight: bfloat16 [5120, 2048], P('tp'), may hold values from -0.078125 to 0.078125
- kv_cache: bfloat16 [32768, 2048], P(('groups', 'tp', 'pool')), parts along dimension 0, may hold values from -6 to 6
- queries: bfloat16 [64, 4096], P(('groups', 'tp', 'pool')), parts along dimension 0, may hold values from -12 to 12
- placement: int32 [64], P('groups'), parts along dimension 0, may hold values from 0 to 31, as said below
- cached_len: int32 [64], P('groups'), parts along dimension 0, may hold values from 64 to 512
- frame_count: int32 [64], P('groups'), parts along dimension 0, may hold values from 1 to 64
Outputs:
- attended: bfloat16 [64, 4096], P(('groups', 'tp', 'pool')), parts along dimension 0
The draws below stay inside these ranges and needn't reach their ends.
There are 2 independent parts, one for each index of `groups`. The reference program is written for one: setup_inputs(seed, part) draws one part's arguments, and reference() takes and returns one part's arrays. A program takes and returns all parts, laid end to end along the dimension named above; an argument that names none is the same for every part. Nothing has to cross between parts.
Inputs may be any that keep to these rules, and one draw needn't show every extreme that they name: placement[s] = owner * 2 + slot, where owner counts devices along tp and pool with tp slowest; no two sessions share a row; the 8 consecutive sessions of one prefill group have different owners, and exactly 2 of them have owners with any given pool index; every owner holds no session or 2 of them.
All inputs are finite; a program needn't handle non-finite values.
Results may differ from the reference program's by a relative error of at most 0.007.
Values may be sent and summed in bfloat16 or wider, within the bound.
A program may use at most 128 MiB of HBM per device.

```python
import jax
import jax.numpy as jnp
from jax import lax

D = 5120
QH = 32
KVH = 8
HD = 128
FRAMES = 64
SLOT_TOK = 512
KVW = 2048
SES_GRP = 8
SESS = 32
OWNERS = 16
SLOT_DEV = 2
CAP_COL = 2
N_TP = 4
N_POOL = 4


def draw_kv_cache(key, part):
    key = jax.random.fold_in(key, 5)
    shape = (OWNERS * SLOT_DEV * SLOT_TOK, KVW)
    values = jnp.clip(jax.random.normal(key, shape, jnp.float32), -6.0, 6.0)
    return values.astype(jnp.bfloat16)


def draw_queries(key, part):
    key = jax.random.fold_in(key, 7)
    shape = (OWNERS * SLOT_DEV, QH * HD)
    values = jnp.clip(2.5 * jax.random.normal(key, shape, jnp.float32), -12.0, 12.0)
    return values.astype(jnp.bfloat16)


def draw_placement(key, part):
    key = jax.random.fold_in(key, 11)
    key_one, key_two, key_three = jax.random.split(key, 3)
    tensor_perm = jax.vmap(lambda k: jax.random.permutation(k, N_TP))(jax.random.split(key_one, N_POOL))
    local_perm = jax.vmap(lambda k: jax.random.permutation(k, SES_GRP))(jax.random.split(key_two, N_POOL))
    slot_perm = jax.vmap(lambda k: jax.random.permutation(k, SLOT_DEV))(jax.random.split(key_three, 2 * SES_GRP))
    session_ids = jnp.arange(SESS, dtype=jnp.int32)
    group_ids = session_ids // SES_GRP
    within = session_ids % SES_GRP
    half = group_ids % 2
    level = group_ids // 2
    shuffled = local_perm[group_ids, within].astype(jnp.int32)
    column = shuffled // CAP_COL
    offset = shuffled % CAP_COL
    tensor_pick = tensor_perm[column, half * CAP_COL + offset].astype(jnp.int32)
    owner = tensor_pick * N_POOL + column
    active = half * SES_GRP + shuffled
    slot_pick = slot_perm[active, level].astype(jnp.int32)
    return (owner * SLOT_DEV + slot_pick).astype(jnp.int32)


def draw_cached_len(key, part):
    key = jax.random.fold_in(key, 13)
    key_one, key_two = jax.random.split(key)
    lengths = jax.random.randint(key_one, (SESS,), max(2, SLOT_TOK // 8), SLOT_TOK + 1, jnp.int32)
    chosen = jax.random.randint(key_two, (), 0, SESS, jnp.int32)
    return jnp.where(jnp.arange(SESS) == chosen, SLOT_TOK, lengths).astype(jnp.int32)


def draw_frame_count(key, part):
    key = jax.random.fold_in(key, 17)
    key_one, key_two = jax.random.split(key)
    counts = jax.random.randint(key_one, (SESS,), 1, FRAMES + 1, jnp.int32)
    chosen = jax.random.randint(key_two, (), 0, SESS, jnp.int32)
    return jnp.where(jnp.arange(SESS) == chosen, FRAMES, counts).astype(jnp.int32)


def level_of(stream_key, shape, cuts, least, high):
    gain, own = 1.0, jax.random.fold_in(stream_key, 6)
    for dim, blocks in cuts:
        draws = jnp.exp(jax.random.uniform(jax.random.fold_in(own, dim), (blocks,), jnp.float32, least / len(cuts), high / len(cuts)))
        gain = gain * jnp.repeat(draws, shape[dim] // blocks).reshape([-1 if axis == dim else 1 for axis in range(len(shape))])
    return gain


def scatter_about(stream_key, dims, scale, bound, cuts=(), held_as=jnp.bfloat16):
    drawn = jax.random.normal(stream_key, dims, jnp.float32) * scale
    if len(cuts) > 0:
        drawn = level_of(stream_key, dims, cuts, -0.22, 0.18) * drawn
    return jnp.clip(drawn, min=-bound, max=bound).astype(held_as)


def setup_inputs(seed: int = 0, part: int = 0) -> dict:
    splits = jax.random.split(jax.random.key(seed), 9)
    part_keys = jax.random.split(jax.random.fold_in(splits[8], part), 9)
    return {
        "frames": scatter_about(part_keys[0], (SESS * FRAMES, D), 1.0, 6.0, ((0, 4), (1, 4))),
        "norm_gain": jnp.clip(1.0 + 0.18 * jax.random.normal(splits[1], (D,), jnp.float32), 0.099609375, 1.8984375).astype(jnp.bfloat16),
        "kv_weight": scatter_about(splits[2], (D, KVW), D ** -0.5, 0.078125, ((0, 4),)),
        "kv_cache": draw_kv_cache(jax.random.fold_in(jax.random.fold_in(splits[8], part), 71), part),
        "queries": draw_queries(jax.random.fold_in(jax.random.fold_in(splits[8], part), 71), part),
        "placement": draw_placement(jax.random.fold_in(jax.random.fold_in(splits[8], part), 71), part),
        "cached_len": draw_cached_len(jax.random.fold_in(jax.random.fold_in(splits[8], part), 71), part),
        "frame_count": draw_frame_count(jax.random.fold_in(jax.random.fold_in(splits[8], part), 71), part),
    }


def attend_slot(queries_row, cached, fresh_rows, cached_count, fresh_count):
    group_size = QH // KVH
    query_heads = queries_row.astype(jnp.float32).reshape(KVH, group_size, HD)
    stacked = jnp.concatenate([cached, fresh_rows], axis=0)
    key_part = stacked[:, :KVH * HD].astype(jnp.float32).reshape(-1, KVH, HD)
    value_part = stacked[:, KVH * HD:].astype(jnp.float32).reshape(-1, KVH, HD)
    scores = jnp.einsum('kgd,tkd->kgt', query_heads, key_part) * HD ** (-0.5)
    positions = jnp.arange(SLOT_TOK + FRAMES)
    usable = jnp.where(positions < SLOT_TOK, positions < cached_count, positions - SLOT_TOK < fresh_count)
    scores = jnp.where(usable, scores, -1e+30)
    highest = lax.optimization_barrier(jnp.max(scores, axis=-1, keepdims=True))
    exponent = jnp.exp(scores - highest)
    denominator = lax.optimization_barrier(jnp.sum(exponent, axis=-1, keepdims=True))
    weights = (exponent / denominator).astype(jnp.bfloat16)
    attended = jnp.einsum('kgt,tkd->kgd', weights.astype(jnp.float32), value_part)
    return attended.reshape(QH * HD).astype(jnp.bfloat16)

def reference(frames, norm_gain, kv_weight, kv_cache, queries, placement, cached_len, frame_count):
    widened = frames.astype(jnp.float32)
    inverse = lax.rsqrt(lax.optimization_barrier(jnp.mean(widened * widened, axis=1)) + 1e-06)
    scaled = (widened * norm_gain.astype(jnp.float32)[None, :]).astype(jnp.bfloat16)
    projected = jnp.dot(scaled, kv_weight, preferred_element_type=jnp.float32)
    fresh_all = (projected * inverse[:, None]).astype(jnp.bfloat16).reshape(-1, FRAMES, KVW)
    cache_slots = kv_cache.reshape(-1, SLOT_TOK, KVW)

    def per_session(session):
        slot_row = placement[session]
        return attend_slot(queries[slot_row], cache_slots[slot_row], fresh_all[session], cached_len[session], frame_count[session])
    results = lax.map(per_session, jnp.arange(placement.shape[0], dtype=jnp.int32))
    output = jnp.zeros((queries.shape[0], QH * HD), jnp.bfloat16).at[placement].set(results)
    return output
```

```python
import functools

import jax
import jax.numpy as jnp
from jax import lax
from jax.experimental import pallas as pl
from jax.experimental.pallas import tpu as pltpu
from jax.sharding import PartitionSpec as P

QH = 32
KVH = 8
HD = 128
GRP = QH // KVH
HS = KVH * HD
FRAMES = 64
SLOT_TOK = 512
PACK = 128 // QH
F32 = jnp.float32
BF = jnp.bfloat16
NT = (((1,), (1,)), ((), ()))
TN = (((0,), (0,)), ((), ()))


def iota(shape, dim):
    return lax.broadcasted_iota(jnp.int32, shape, dim)


def spread_heads(rows):
    wide = jnp.concatenate([rows.astype(F32)] * KVH, axis=1)
    own = (iota(wide.shape, 0) % QH) // GRP == iota(wide.shape, 1) // HD
    return jnp.where(own, wide, 0.0).astype(BF)


def gather_heads(wide):
    head = (iota((wide.shape[0], HD), 0) % QH) // GRP
    out = jnp.zeros((wide.shape[0], HD), F32)
    for j in range(KVH):
        out = jnp.where(head == j, wide[:, j * HD:(j + 1) * HD], out)
    return out


def permute(picks, blocks):
    shape = (QH, blocks.shape[0])
    offset = iota(shape, 1) - iota(shape, 0)
    hot = jnp.concatenate([jnp.where(offset == pick * QH, 1.0, 0.0) for pick in picks], axis=0)
    return jnp.dot(hot.astype(BF), blocks, preferred_element_type=F32).astype(BF)


def kernel(n_tp, n_pool, place, clen, fcnt, gain, q, frames_h, w_h, cache_h, out,
           fr, wk, wv, ca, xs, qt, qg, sendq, recvq, ssq, sg, lse, ob, sendo, recvo,
           sendp, recvp, oc,
           ld, s_tp, r_tp, s_pl, r_pl):
    slots = q.shape[0] // QH
    n_loc = fr.shape[0] // FRAMES
    per = n_loc // n_pool
    tiles = n_loc // PACK
    width = fr.shape[1]
    scale = HD ** -0.5
    t = lax.axis_index("tp")
    p = lax.axis_index("pool")

    loads = [
        pltpu.make_async_copy(frames_h, fr, ld.at[0]),
        pltpu.make_async_copy(w_h.at[:, pl.ds(0, HS)], wk, ld.at[1]),
        pltpu.make_async_copy(cache_h, ca, ld.at[2]),
        pltpu.make_async_copy(w_h.at[:, pl.ds(HS, HS)], wv, ld.at[3]),
    ]
    for c in loads:
        c.start()

    barrier = pltpu.get_barrier_semaphore()
    for d in range(1, n_tp):
        pl.semaphore_signal(barrier, inc=1, device_id={"tp": lax.rem(t + d, n_tp)},
                            device_id_type=pl.DeviceIdType.MESH)
    for d in range(1, n_pool):
        pl.semaphore_signal(barrier, inc=1, device_id={"pool": lax.rem(p + d, n_pool)},
                            device_id_type=pl.DeviceIdType.MESH)

    def to_tp(stage, src, dst):
        made = []
        for d in range(1, n_tp):
            peer = lax.rem(t + d, n_tp)
            made.append(pltpu.make_async_remote_copy(
                src_ref=src(peer), dst_ref=dst, send_sem=s_tp.at[stage, d],
                recv_sem=r_tp.at[stage, d], device_id={"tp": peer},
                device_id_type=pl.DeviceIdType.MESH))
        for c in made:
            c.start()
        return made

    def to_pool(stage, src, dst):
        made = []
        for d in range(1, n_pool):
            peer = lax.rem(p + d, n_pool)
            made.append(pltpu.make_async_remote_copy(
                src_ref=src(peer), dst_ref=dst, send_sem=s_pl.at[stage, d],
                recv_sem=r_pl.at[stage, d], device_id={"pool": peer},
                device_id_type=pl.DeviceIdType.MESH))
        for c in made:
            c.start()
        return made

    qg[t] = q[...]
    pl.semaphore_wait(barrier, n_tp - 1 + n_pool - 1)
    hop = to_tp(0, lambda peer: qg.at[t], qg.at[t])

    keys = []
    for g in range(n_pool):
        found = [jnp.int32(0)] * per
        count = jnp.int32(0)
        for s in range(g * n_loc, (g + 1) * n_loc):
            row = place[s]
            owner = row // slots
            match = owner % n_pool == p
            key = (owner // n_pool) * slots + row % slots
            for k in range(per):
                found[k] = jnp.where(match & (count == k), key, found[k])
            count = count + match.astype(jnp.int32)
        keys += found
    held = []
    for o in range(n_tp * slots):
        which = jnp.int32(-1)
        for c in range(n_pool * per):
            which = jnp.where(keys[c] == o, c, which)
        held.append(which)
    counts = [jnp.int32(0)] * n_pool
    order = [jnp.int32(0)] * n_loc
    for s in range(n_loc):
        column = (place[p * n_loc + s] // slots) % n_pool
        for c in range(n_pool):
            match = column == c
            for k in range(per):
                u = c * per + k
                order[u] = jnp.where(match & (counts[c] == k), s, order[u])
            counts[c] = counts[c] + match.astype(jnp.int32)
    lengths, mine = [], []
    for i in range(slots):
        length = jnp.int32(0)
        for s in range(n_pool * n_loc):
            length = jnp.where(place[s] == (t * n_pool + p) * slots + i, clen[s], length)
        which = jnp.int32(-1)
        for c in range(n_pool * per):
            which = jnp.where(keys[c] == t * slots + i, c, which)
        lengths.append(length)
        mine.append(which)

    loads[0].wait()
    gain_row = gain[...].astype(F32)
    lane = iota((FRAMES, 128), 1)

    def scale_session(s, total):
        x = fr[s * FRAMES:(s + 1) * FRAMES, :].astype(F32)
        xs[s * FRAMES:(s + 1) * FRAMES, :] = (x * gain_row).astype(BF)
        return jnp.where(lane == s, jnp.sum(x * x, axis=1, keepdims=True), total)

    total = jnp.zeros((FRAMES, 128), F32)
    for s in range(n_loc // 2):
        total = scale_session(s, total)

    for c in hop:
        c.wait()
    moved = permute(keys, qg[...].reshape(n_tp * slots * QH, HD))
    sendq[...] = moved.reshape(n_pool, per * QH, HD)
    recvq[p] = sendq[p]
    hop = to_pool(0, lambda peer: sendq.at[peer], recvq.at[p])

    for s in range(n_loc // 2, n_loc):
        total = scale_session(s, total)
    ssq[t] = total
    hop_sq = to_tp(1, lambda peer: ssq.at[t], ssq.at[t])
    loads[1].wait()
    for c in hop:
        c.wait()

    who = []
    group = recvq[...].reshape(n_loc * QH, HD)
    for a in range(tiles):
        ids = jnp.zeros((FRAMES, 128), jnp.int32)
        for k in range(PACK):
            ids = jnp.where(lane // QH == k, order[a * PACK + k], ids)
        who.append(ids)
        qt[:, a * 128:(a + 1) * 128] = lax.dot_general(
            wk[...], spread_heads(group[a * 128:(a + 1) * 128]), NT,
            preferred_element_type=F32).astype(BF)
    full = jnp.dot(xs[...], qt[...], preferred_element_type=F32)
    for a in range(tiles):
        packed = jnp.zeros((FRAMES, 128), F32)
        for s in range(n_loc):
            packed = jnp.where(who[a] == s, full[s * FRAMES:(s + 1) * FRAMES, a * 128:(a + 1) * 128],
                               packed)
        sg[t, a * FRAMES:(a + 1) * FRAMES, :] = packed
    hop = to_tp(2, lambda peer: sg.at[t], sg.at[t])

    loads[2].wait()
    tops, sums = [], []
    for i in range(slots):
        qb = spread_heads(q[i * QH:(i + 1) * QH, :])
        rows = slice(i * SLOT_TOK, (i + 1) * SLOT_TOK)
        sc = lax.dot_general(qb, ca[rows, :HS], NT, preferred_element_type=F32) * scale
        sc = jnp.where(iota(sc.shape, 1) < lengths[i], sc, -1e30)
        top = jnp.max(sc, axis=1, keepdims=True)
        pr = jnp.exp(sc - top)
        tops.append(top)
        sums.append(jnp.sum(pr, axis=1, keepdims=True))
        oc[i * QH:(i + 1) * QH, :] = gather_heads(
            jnp.dot(pr.astype(BF), ca[rows, HS:], preferred_element_type=F32))

    for c in hop_sq:
        c.wait()
    squares = ssq[0]
    for j in range(1, n_tp):
        squares = squares + ssq[j]
    inverse = lax.rsqrt(squares / (width * n_tp) + 1e-06)
    for c in hop:
        c.wait()
    weights = []
    for a in range(tiles):
        inv = jnp.zeros((FRAMES, 128), F32)
        valid = jnp.zeros((FRAMES, 128), jnp.int32)
        for s in range(n_loc):
            inv = jnp.where(who[a] == s, inverse[:, s:s + 1], inv)
            valid = jnp.where(who[a] == s, fcnt[p * n_loc + s], valid)
        sc = sg[0, a * FRAMES:(a + 1) * FRAMES, :]
        for j in range(1, n_tp):
            sc = sc + sg[j, a * FRAMES:(a + 1) * FRAMES, :]
        sc = jnp.where(iota(sc.shape, 0) < valid, sc * (inv * scale), -1e30)
        top = jnp.max(sc, axis=0, keepdims=True)
        pr = jnp.exp(sc - top)
        norm = jnp.sum(pr, axis=0, keepdims=True)
        lse[p, a:a + 1, :] = top + jnp.log(norm)
        weights.append(pr * inv / norm)
    if tiles < lse.shape[1]:
        lse[p, tiles:, :] = jnp.zeros((lse.shape[1] - tiles, 128), F32)
    hop_l = to_pool(1, lambda peer: lse.at[p], lse.at[p])

    loads[3].wait()
    for a in range(tiles):
        wide = jnp.concatenate(
            [jnp.where(who[a] == s, weights[a], 0.0) for s in range(n_loc)], axis=0)
        y = jnp.dot(wide.T.astype(BF), xs[...], preferred_element_type=F32).astype(BF)
        ob[a * 128:(a + 1) * 128, :] = gather_heads(
            jnp.dot(y, wv[...], preferred_element_type=F32)).astype(BF)
    sendo[...] = ob[...].reshape(n_pool, per * QH, HD)
    recvo[p] = sendo[p]
    hop = to_pool(2, lambda peer: sendo.at[peer], recvo.at[p])
    for c in hop_l:
        c.wait()
    fresh_lse = []
    offset = iota((QH, 128), 1) - iota((QH, 128), 0)
    for i in range(slots):
        spread = jnp.zeros((QH, 128), F32)
        for c in range(n_pool * per):
            u = p * per + c % per
            line = lse[c // per, pl.ds(u // PACK, 1), :]
            here = (offset == (u % PACK) * QH) & (mine[i] == c)
            spread = jnp.where(here, line, spread)
        fresh_lse.append(jnp.sum(spread, axis=1, keepdims=True))
    for c in hop:
        c.wait()

    moved = permute(held, recvo[...].reshape(n_loc * QH, HD))
    sendp[...] = moved.reshape(n_tp, slots * QH, HD)
    recvp[t] = sendp[t]
    hop = to_tp(3, lambda peer: sendp.at[peer], recvp.at[t])
    for c in hop:
        c.wait()
    for i in range(slots):
        rows = slice(i * QH, (i + 1) * QH)
        new = recvp[0, rows, :].astype(F32)
        for j in range(1, n_tp):
            new = new + recvp[j, rows, :].astype(F32)
        top = jnp.maximum(tops[i], fresh_lse[i])
        ea = jnp.exp(fresh_lse[i] - top)
        eb = jnp.exp(tops[i] - top)
        res = (ea * new + eb * oc[rows, :]) / (ea + eb * sums[i])
        out[rows, :] = jnp.where(mine[i] >= 0, res, 0.0).astype(BF)


def per_device(n_tp, n_pool, frames, norm_gain, kv_weight, kv_cache, queries, placement,
               cached_len, frame_count):
    rows, width = frames.shape
    slots = queries.shape[0]
    n_loc = rows // FRAMES
    per = n_loc // n_pool
    tiles = n_loc // PACK
    vm = pl.BlockSpec(memory_space=pltpu.VMEM)
    sm = pl.BlockSpec(memory_space=pltpu.SMEM)
    hbm = pl.BlockSpec(memory_space=pltpu.HBM)
    out = pl.pallas_call(
        functools.partial(kernel, n_tp, n_pool),
        out_shape=jax.ShapeDtypeStruct((slots * QH, HD), BF),
        in_specs=[sm, sm, sm, vm, vm, hbm, hbm, hbm],
        out_specs=vm,
        scratch_shapes=[
            pltpu.VMEM((rows, width), BF),
            pltpu.VMEM((width, HS), BF),
            pltpu.VMEM((width, HS), BF),
            pltpu.VMEM(kv_cache.shape, BF),
            pltpu.VMEM((rows, width), BF),
            pltpu.VMEM((width, n_loc * QH), BF),
            pltpu.VMEM((n_tp, slots * QH, HD), BF),
            pltpu.VMEM((n_pool, per * QH, HD), BF),
            pltpu.VMEM((n_pool, per * QH, HD), BF),
            pltpu.VMEM((n_tp, FRAMES, 128), F32),
            pltpu.VMEM((n_tp, tiles * FRAMES, 128), F32),
            pltpu.VMEM((n_pool, max(8, tiles), 128), F32),
            pltpu.VMEM((n_loc * QH, HD), BF),
            pltpu.VMEM((n_pool, per * QH, HD), BF),
            pltpu.VMEM((n_pool, per * QH, HD), BF),
            pltpu.VMEM((n_tp, slots * QH, HD), BF),
            pltpu.VMEM((n_tp, slots * QH, HD), BF),
            pltpu.VMEM((slots * QH, HD), F32),
            pltpu.SemaphoreType.DMA((4,)),
            pltpu.SemaphoreType.DMA((4, n_tp)),
            pltpu.SemaphoreType.DMA((4, n_tp)),
            pltpu.SemaphoreType.DMA((3, n_pool)),
            pltpu.SemaphoreType.DMA((3, n_pool)),
        ],
        compiler_params=pltpu.CompilerParams(
            collective_id=0, has_side_effects=True, vmem_limit_bytes=62 * 1024 * 1024),
    )(placement, cached_len, frame_count, norm_gain.reshape(1, width),
      queries.reshape(slots * QH, HD), frames, kv_weight, kv_cache)
    return out.reshape(slots, QH * HD)


def solution(mesh):
    return jax.shard_map(
        functools.partial(per_device, mesh.shape["tp"], mesh.shape["pool"]),
        mesh=mesh,
        in_specs=(
            P(("groups", "pool"), "tp"),
            P("tp"),
            P("tp", None),
            P(("groups", "tp", "pool"), None),
            P(("groups", "tp", "pool"), None),
            P("groups"),
            P("groups"),
            P("groups"),
        ),
        out_specs=P(("groups", "tp", "pool"), None),
        check_vma=False,
    )
```

```python
import functools

import jax
import jax.numpy as jnp
from jax import lax
from jax.experimental import pallas as pl
from jax.experimental.pallas import tpu as pltpu
from jax.sharding import PartitionSpec as P

QH = 32
KVH = 8
HD = 128
GRP = QH // KVH
HS = KVH * HD
FRAMES = 64
SLOT_TOK = 512
PACK = 128 // QH
F32 = jnp.float32
BF = jnp.bfloat16
NT = (((1,), (1,)), ((), ()))
TN = (((0,), (0,)), ((), ()))


def iota(shape, dim):
    return lax.broadcasted_iota(jnp.int32, shape, dim)


def spread_heads(rows):
    wide = jnp.concatenate([rows.astype(F32)] * KVH, axis=1)
    own = (iota(wide.shape, 0) % QH) // GRP == iota(wide.shape, 1) // HD
    return jnp.where(own, wide, 0.0).astype(BF)


def gather_heads(wide):
    head = (iota((wide.shape[0], HD), 0) % QH) // GRP
    out = jnp.zeros((wide.shape[0], HD), F32)
    for j in range(KVH):
        out = jnp.where(head == j, wide[:, j * HD:(j + 1) * HD], out)
    return out


def permute(picks, blocks):
    shape = (QH, blocks.shape[0])
    offset = iota(shape, 1) - iota(shape, 0)
    hot = jnp.concatenate([jnp.where(offset == pick * QH, 1.0, 0.0) for pick in picks], axis=0)
    return jnp.dot(hot.astype(BF), blocks, preferred_element_type=F32).astype(BF)


def kernel(n_tp, n_pool, place, clen, fcnt, gain, q, frames_h, w_h, cache_h, out,
           fr, wk, wv, ca, xs, qt, qg, sendq, recvq, ssq, sg, lse, sendo, recvo,
           sendp, recvp, oc,
           ld, s_tp, r_tp, s_pl, r_pl):
    slots = q.shape[0]
    n_loc = fr.shape[0] // FRAMES
    per = n_loc // n_pool
    tiles = n_loc // PACK
    width = fr.shape[1]
    scale = HD ** -0.5
    t = lax.axis_index("tp")
    p = lax.axis_index("pool")

    loads = [
        pltpu.make_async_copy(frames_h, fr, ld.at[0]),
        pltpu.make_async_copy(w_h.at[:, pl.ds(0, HS)], wk, ld.at[1]),
        pltpu.make_async_copy(cache_h, ca, ld.at[2]),
        pltpu.make_async_copy(w_h.at[:, pl.ds(HS, HS)], wv, ld.at[3]),
    ]
    for c in loads:
        c.start()

    barrier = pltpu.get_barrier_semaphore()
    for d in range(1, n_tp):
        pl.semaphore_signal(barrier, inc=1, device_id={"tp": lax.rem(t + d, n_tp)},
                            device_id_type=pl.DeviceIdType.MESH)
    for d in range(1, n_pool):
        pl.semaphore_signal(barrier, inc=1, device_id={"pool": lax.rem(p + d, n_pool)},
                            device_id_type=pl.DeviceIdType.MESH)

    def to_tp(stage, src, dst):
        made = []
        for d in range(1, n_tp):
            peer = lax.rem(t + d, n_tp)
            made.append(pltpu.make_async_remote_copy(
                src_ref=src(peer), dst_ref=dst, send_sem=s_tp.at[stage, d],
                recv_sem=r_tp.at[stage, d], device_id={"tp": peer},
                device_id_type=pl.DeviceIdType.MESH))
        for c in made:
            c.start()
        return made

    def to_pool(stage, src, dst):
        made = []
        for d in range(1, n_pool):
            peer = lax.rem(p + d, n_pool)
            made.append(pltpu.make_async_remote_copy(
                src_ref=src(peer), dst_ref=dst, send_sem=s_pl.at[stage, d],
                recv_sem=r_pl.at[stage, d], device_id={"pool": peer},
                device_id_type=pl.DeviceIdType.MESH))
        for c in made:
            c.start()
        return made

    rows = [q[i:i + 1, h * HD:(h + 1) * HD].astype(F32) for i in range(slots) for h in range(QH)]
    qg[t] = jnp.concatenate(rows, axis=0).astype(BF)
    pl.semaphore_wait(barrier, n_tp - 1 + n_pool - 1)
    hop = to_tp(0, lambda peer: qg.at[t], qg.at[t])

    keys = []
    for g in range(n_pool):
        found = [jnp.int32(0)] * per
        count = jnp.int32(0)
        for s in range(g * n_loc, (g + 1) * n_loc):
            row = place[s]
            owner = row // slots
            match = owner % n_pool == p
            key = (owner // n_pool) * slots + row % slots
            for k in range(per):
                found[k] = jnp.where(match & (count == k), key, found[k])
            count = count + match.astype(jnp.int32)
        keys += found
    held = []
    for o in range(n_tp * slots):
        which = jnp.int32(-1)
        for c in range(n_pool * per):
            which = jnp.where(keys[c] == o, c, which)
        held.append(which)
    counts = [jnp.int32(0)] * n_pool
    order = [jnp.int32(0)] * n_loc
    for s in range(n_loc):
        column = (place[p * n_loc + s] // slots) % n_pool
        for c in range(n_pool):
            match = column == c
            for k in range(per):
                u = c * per + k
                order[u] = jnp.where(match & (counts[c] == k), s, order[u])
            counts[c] = counts[c] + match.astype(jnp.int32)
    lengths, mine = [], []
    for i in range(slots):
        length = jnp.int32(0)
        for s in range(n_pool * n_loc):
            length = jnp.where(place[s] == (t * n_pool + p) * slots + i, clen[s], length)
        which = jnp.int32(-1)
        for c in range(n_pool * per):
            which = jnp.where(keys[c] == t * slots + i, c, which)
        lengths.append(length)
        mine.append(which)

    loads[0].wait()
    gain_row = gain[...].astype(F32).reshape(1, width)
    lane = iota((FRAMES, 128), 1)

    def scale_session(s, total):
        x = fr[s * FRAMES:(s + 1) * FRAMES, :].astype(F32)
        xs[s * FRAMES:(s + 1) * FRAMES, :] = (x * gain_row).astype(BF)
        return jnp.where(lane == s, jnp.sum(x * x, axis=1, keepdims=True), total)

    total = jnp.zeros((FRAMES, 128), F32)
    for s in range(n_loc // 2):
        total = scale_session(s, total)

    for c in hop:
        c.wait()
    moved = permute(keys, qg[...].reshape(n_tp * slots * QH, HD))
    sendq[...] = moved.reshape(n_pool, per * QH, HD)
    recvq[p] = sendq[p]
    hop = to_pool(0, lambda peer: sendq.at[peer], recvq.at[p])

    for s in range(n_loc // 2, n_loc):
        total = scale_session(s, total)
    ssq[t] = total.T[:n_loc]
    hop_sq = to_tp(1, lambda peer: ssq.at[t], ssq.at[t])
    loads[1].wait()
    for c in hop:
        c.wait()

    who = []
    group = recvq[...].reshape(n_loc * QH, HD)
    for a in range(tiles):
        ids = jnp.zeros((FRAMES, 128), jnp.int32)
        for k in range(PACK):
            ids = jnp.where(lane // QH == k, order[a * PACK + k], ids)
        who.append(ids)
    qt[...] = lax.dot_general(wk[...], spread_heads(group), NT,
                              preferred_element_type=F32).astype(BF)
    full = jnp.dot(xs[...], qt[...], preferred_element_type=F32)
    for a in range(tiles):
        packed = jnp.zeros((FRAMES, 128), F32)
        for s in range(n_loc):
            packed = jnp.where(who[a] == s, full[s * FRAMES:(s + 1) * FRAMES, a * 128:(a + 1) * 128],
                               packed)
        sg[t, a * FRAMES:(a + 1) * FRAMES, :] = packed.astype(BF)
    hop = to_tp(2, lambda peer: sg.at[t], sg.at[t])

    loads[2].wait()
    tops, sums = [], []
    for i in range(slots):
        qb = spread_heads(qg[t, i * QH:(i + 1) * QH, :])
        rows = slice(i * SLOT_TOK, (i + 1) * SLOT_TOK)
        sc = lax.dot_general(qb, ca[rows, :HS], NT, preferred_element_type=F32) * scale
        sc = jnp.where(iota(sc.shape, 1) < lengths[i], sc, -1e30)
        top = jnp.max(sc, axis=1, keepdims=True)
        pr = jnp.exp(sc - top)
        tops.append(top)
        sums.append(jnp.sum(pr, axis=1, keepdims=True))
        oc[i * QH:(i + 1) * QH, :] = gather_heads(
            jnp.dot(pr.astype(BF), ca[rows, HS:], preferred_element_type=F32))

    for c in hop_sq:
        c.wait()
    squares = ssq[0]
    for j in range(1, n_tp):
        squares = squares + ssq[j]
    inverse = lax.rsqrt(squares / (width * n_tp) + 1e-06)
    inverse = jnp.concatenate([inverse, jnp.zeros((128 - n_loc, FRAMES), F32)], axis=0).T
    for c in hop:
        c.wait()
    weights = []
    for a in range(tiles):
        inv = jnp.zeros((FRAMES, 128), F32)
        valid = jnp.zeros((FRAMES, 128), jnp.int32)
        for s in range(n_loc):
            inv = jnp.where(who[a] == s, inverse[:, s:s + 1], inv)
            valid = jnp.where(who[a] == s, fcnt[p * n_loc + s], valid)
        sc = sg[0, a * FRAMES:(a + 1) * FRAMES, :].astype(F32)
        for j in range(1, n_tp):
            sc = sc + sg[j, a * FRAMES:(a + 1) * FRAMES, :].astype(F32)
        sc = jnp.where(iota(sc.shape, 0) < valid, sc * (inv * scale), -1e30)
        top = jnp.max(sc, axis=0, keepdims=True)
        pr = jnp.exp(sc - top)
        norm = jnp.sum(pr, axis=0, keepdims=True)
        lse[p, a:a + 1, :] = top + jnp.log(norm)
        weights.append(pr * inv / norm)
    if tiles < lse.shape[1]:
        lse[p, tiles:, :] = jnp.zeros((lse.shape[1] - tiles, 128), F32)
    hop_l = to_pool(1, lambda peer: lse.at[p], lse.at[p])

    loads[3].wait()
    wide = jnp.concatenate(
        [jnp.concatenate([jnp.where(who[a] == s, weights[a], 0.0) for s in range(n_loc)], axis=0).T
         for a in range(tiles)], axis=0)
    y = jnp.dot(wide.astype(BF), xs[...], preferred_element_type=F32).astype(BF)
    ob = gather_heads(jnp.dot(y, wv[...], preferred_element_type=F32)).astype(BF)
    sendo[...] = ob.reshape(n_pool, per * QH, HD)
    recvo[p] = sendo[p]
    hop = to_pool(2, lambda peer: sendo.at[peer], recvo.at[p])
    for c in hop_l:
        c.wait()
    fresh_lse = []
    offset = iota((QH, 128), 1) - iota((QH, 128), 0)
    for i in range(slots):
        spread = jnp.zeros((QH, 128), F32)
        for c in range(n_pool * per):
            u = p * per + c % per
            line = lse[c // per, pl.ds(u // PACK, 1), :]
            here = (offset == (u % PACK) * QH) & (mine[i] == c)
            spread = jnp.where(here, line, spread)
        fresh_lse.append(jnp.sum(spread, axis=1, keepdims=True))
    for c in hop:
        c.wait()

    moved = permute(held, recvo[...].reshape(n_loc * QH, HD))
    sendp[...] = moved.reshape(n_tp, slots * QH, HD)
    recvp[t] = sendp[t]
    hop = to_tp(3, lambda peer: sendp.at[peer], recvp.at[t])
    for c in hop:
        c.wait()
    for i in range(slots):
        rows = slice(i * QH, (i + 1) * QH)
        new = recvp[0, rows, :].astype(F32)
        for j in range(1, n_tp):
            new = new + recvp[j, rows, :].astype(F32)
        top = jnp.maximum(tops[i], fresh_lse[i])
        ea = jnp.exp(fresh_lse[i] - top)
        eb = jnp.exp(tops[i] - top)
        res = (ea * new + eb * oc[rows, :]) / (ea + eb * sums[i])
        out[rows, :] = jnp.where(mine[i] >= 0, res, 0.0).astype(BF)


def per_device(n_tp, n_pool, frames, norm_gain, kv_weight, kv_cache, queries, placement,
               cached_len, frame_count):
    rows, width = frames.shape
    slots = queries.shape[0]
    n_loc = rows // FRAMES
    per = n_loc // n_pool
    tiles = n_loc // PACK
    vm = pl.BlockSpec(memory_space=pltpu.VMEM)
    sm = pl.BlockSpec(memory_space=pltpu.SMEM)
    hbm = pl.BlockSpec(memory_space=pltpu.HBM)
    out = pl.pallas_call(
        functools.partial(kernel, n_tp, n_pool),
        out_shape=jax.ShapeDtypeStruct((slots * QH, HD), BF),
        in_specs=[sm, sm, sm, vm, vm, hbm, hbm, hbm],
        out_specs=vm,
        scratch_shapes=[
            pltpu.VMEM((rows, width), BF),
            pltpu.VMEM((width, HS), BF),
            pltpu.VMEM((width, HS), BF),
            pltpu.VMEM(kv_cache.shape, BF),
            pltpu.VMEM((rows, width), BF),
            pltpu.VMEM((width, n_loc * QH), BF),
            pltpu.VMEM((n_tp, slots * QH, HD), BF),
            pltpu.VMEM((n_pool, per * QH, HD), BF),
            pltpu.VMEM((n_pool, per * QH, HD), BF),
            pltpu.VMEM((n_tp, n_loc, FRAMES), F32),
            pltpu.VMEM((n_tp, tiles * FRAMES, 128), BF),
            pltpu.VMEM((n_pool, max(8, tiles), 128), F32),
            pltpu.VMEM((n_pool, per * QH, HD), BF),
            pltpu.VMEM((n_pool, per * QH, HD), BF),
            pltpu.VMEM((n_tp, slots * QH, HD), BF),
            pltpu.VMEM((n_tp, slots * QH, HD), BF),
            pltpu.VMEM((slots * QH, HD), F32),
            pltpu.SemaphoreType.DMA((4,)),
            pltpu.SemaphoreType.DMA((4, n_tp)),
            pltpu.SemaphoreType.DMA((4, n_tp)),
            pltpu.SemaphoreType.DMA((3, n_pool)),
            pltpu.SemaphoreType.DMA((3, n_pool)),
        ],
        compiler_params=pltpu.CompilerParams(
            collective_id=0, has_side_effects=True, vmem_limit_bytes=62 * 1024 * 1024),
    )(placement, cached_len, frame_count, norm_gain,
      queries, frames, kv_weight, kv_cache)
    return out.reshape(slots, QH * HD)


def solution(mesh):
    return jax.shard_map(
        functools.partial(per_device, mesh.shape["tp"], mesh.shape["pool"]),
        mesh=mesh,
        in_specs=(
            P(("groups", "pool"), "tp"),
            P("tp"),
            P("tp", None),
            P(("groups", "tp", "pool"), None),
            P(("groups", "tp", "pool"), None),
            P("groups"),
            P("groups"),
            P("groups"),
        ),
        out_specs=P(("groups", "tp", "pool"), None),
        check_vma=False,
    )
```

```python
import functools

import jax
import jax.numpy as jnp
from jax import lax
from jax.experimental import pallas as pl
from jax.experimental.pallas import tpu as pltpu
from jax.sharding import PartitionSpec as P

QH = 32
KVH = 8
HD = 128
GRP = QH // KVH
HS = KVH * HD
FRAMES = 64
SLOT_TOK = 512
PACK = 128 // QH
F32 = jnp.float32
BF = jnp.bfloat16
NT = (((1,), (1,)), ((), ()))
TN = (((0,), (0,)), ((), ()))


def iota(shape, dim):
    return lax.broadcasted_iota(jnp.int32, shape, dim)


def spread_heads(rows):
    wide = jnp.concatenate([rows.astype(F32)] * KVH, axis=1)
    own = (iota(wide.shape, 0) % QH) // GRP == iota(wide.shape, 1) // HD
    return jnp.where(own, wide, 0.0).astype(BF)


def gather_heads(wide):
    head = (iota((wide.shape[0], HD), 0) % QH) // GRP
    out = jnp.zeros((wide.shape[0], HD), F32)
    for j in range(KVH):
        out = jnp.where(head == j, wide[:, j * HD:(j + 1) * HD], out)
    return out


def permute(picks, blocks):
    shape = (QH, blocks.shape[0])
    offset = iota(shape, 1) - iota(shape, 0)
    hot = jnp.concatenate([jnp.where(offset == pick * QH, 1.0, 0.0) for pick in picks], axis=0)
    return jnp.dot(hot.astype(BF), blocks, preferred_element_type=F32).astype(BF)


def kernel(n_tp, n_pool, place, clen, fcnt, gain, q, frames_h, w_h, cache_h, out,
           fr, wk, wv, ca, xs, kp, vp, qg, sendq, recvq, ssq, sg, lse, sendo, recvo,
           sendp, recvp, oc,
           ld, s_tp, r_tp, s_pl, r_pl):
    slots = q.shape[0]
    n_loc = fr.shape[0] // FRAMES
    per = n_loc // n_pool
    tiles = n_loc // PACK
    width = fr.shape[1]
    scale = HD ** -0.5
    t = lax.axis_index("tp")
    p = lax.axis_index("pool")

    loads = [
        pltpu.make_async_copy(frames_h, fr, ld.at[0]),
        pltpu.make_async_copy(w_h.at[:, pl.ds(0, HS)], wk, ld.at[1]),
        pltpu.make_async_copy(cache_h, ca, ld.at[2]),
        pltpu.make_async_copy(w_h.at[:, pl.ds(HS, HS)], wv, ld.at[3]),
    ]
    for c in loads:
        c.start()

    barrier = pltpu.get_barrier_semaphore()
    for d in range(1, n_tp):
        pl.semaphore_signal(barrier, inc=1, device_id={"tp": lax.rem(t + d, n_tp)},
                            device_id_type=pl.DeviceIdType.MESH)
    for d in range(1, n_pool):
        pl.semaphore_signal(barrier, inc=1, device_id={"pool": lax.rem(p + d, n_pool)},
                            device_id_type=pl.DeviceIdType.MESH)

    def to_tp(stage, src, dst):
        made = []
        for d in range(1, n_tp):
            peer = lax.rem(t + d, n_tp)
            made.append(pltpu.make_async_remote_copy(
                src_ref=src(peer), dst_ref=dst, send_sem=s_tp.at[stage, d],
                recv_sem=r_tp.at[stage, d], device_id={"tp": peer},
                device_id_type=pl.DeviceIdType.MESH))
        for c in made:
            c.start()
        return made

    def to_pool(stage, src, dst):
        made = []
        for d in range(1, n_pool):
            peer = lax.rem(p + d, n_pool)
            made.append(pltpu.make_async_remote_copy(
                src_ref=src(peer), dst_ref=dst, send_sem=s_pl.at[stage, d],
                recv_sem=r_pl.at[stage, d], device_id={"pool": peer},
                device_id_type=pl.DeviceIdType.MESH))
        for c in made:
            c.start()
        return made

    rows = [q[i:i + 1, h * HD:(h + 1) * HD].astype(F32) for i in range(slots) for h in range(QH)]
    qg[t] = jnp.concatenate(rows, axis=0).astype(BF)
    pl.semaphore_wait(barrier, n_tp - 1 + n_pool - 1)
    hop = to_tp(0, lambda peer: qg.at[t], qg.at[t])

    keys = []
    for g in range(n_pool):
        found = [jnp.int32(0)] * per
        count = jnp.int32(0)
        for s in range(g * n_loc, (g + 1) * n_loc):
            row = place[s]
            owner = row // slots
            match = owner % n_pool == p
            key = (owner // n_pool) * slots + row % slots
            for k in range(per):
                found[k] = jnp.where(match & (count == k), key, found[k])
            count = count + match.astype(jnp.int32)
        keys += found
    loads[0].wait()
    gain_row = gain[...].astype(F32).reshape(1, width)
    lane = iota((FRAMES, 128), 1)

    def scale_session(s, total):
        x = fr[s * FRAMES:(s + 1) * FRAMES, :].astype(F32)
        xs[s * FRAMES:(s + 1) * FRAMES, :] = (x * gain_row).astype(BF)
        return jnp.where(lane == s, jnp.sum(x * x, axis=1, keepdims=True), total)

    total = jnp.zeros((FRAMES, 128), F32)
    for s in range(n_loc):
        total = scale_session(s, total)

    ssq[t] = total.T[:n_loc]
    hop_sq = to_tp(1, lambda peer: ssq.at[t], ssq.at[t])
    for c in hop:
        c.wait()
    moved = permute(keys, qg[...].reshape(n_tp * slots * QH, HD))
    sendq[...] = moved.reshape(n_pool, per * QH, HD)
    recvq[p] = sendq[p]
    hop = to_pool(0, lambda peer: sendq.at[peer], recvq.at[p])

    held = []
    for o in range(n_tp * slots):
        which = jnp.int32(-1)
        for c in range(n_pool * per):
            which = jnp.where(keys[c] == o, c, which)
        held.append(which)
    counts = [jnp.int32(0)] * n_pool
    order = [jnp.int32(0)] * n_loc
    for s in range(n_loc):
        column = (place[p * n_loc + s] // slots) % n_pool
        for c in range(n_pool):
            match = column == c
            for k in range(per):
                u = c * per + k
                order[u] = jnp.where(match & (counts[c] == k), s, order[u])
            counts[c] = counts[c] + match.astype(jnp.int32)
    lengths, mine = [], []
    for i in range(slots):
        length = jnp.int32(0)
        for s in range(n_pool * n_loc):
            length = jnp.where(place[s] == (t * n_pool + p) * slots + i, clen[s], length)
        which = jnp.int32(-1)
        for c in range(n_pool * per):
            which = jnp.where(keys[c] == t * slots + i, c, which)
        lengths.append(length)
        mine.append(which)

    loads[1].wait()
    for s in range(0, n_loc, PACK):
        rows = slice(s * FRAMES, (s + PACK) * FRAMES)
        kp[rows, :] = jnp.dot(xs[rows, :], wk[...], preferred_element_type=F32).astype(BF)
    for c in hop:
        c.wait()

    who = []
    group = recvq[...].reshape(n_loc * QH, HD)
    for a in range(tiles):
        ids = jnp.zeros((FRAMES, 128), jnp.int32)
        for k in range(PACK):
            ids = jnp.where(lane // QH == k, order[a * PACK + k], ids)
        who.append(ids)
    full = lax.dot_general(kp[...], spread_heads(group), NT, preferred_element_type=F32)
    for a in range(tiles):
        packed = jnp.zeros((FRAMES, 128), F32)
        for s in range(n_loc):
            packed = jnp.where(who[a] == s, full[s * FRAMES:(s + 1) * FRAMES, a * 128:(a + 1) * 128],
                               packed)
        sg[t, a * FRAMES:(a + 1) * FRAMES, :] = packed.astype(BF)
    hop = to_tp(2, lambda peer: sg.at[t], sg.at[t])

    loads[3].wait()
    for s in range(0, n_loc, PACK):
        rows = slice(s * FRAMES, (s + PACK) * FRAMES)
        vp[rows, :] = jnp.dot(xs[rows, :], wv[...], preferred_element_type=F32).astype(BF)

    for c in hop_sq:
        c.wait()
    squares = ssq[0]
    for j in range(1, n_tp):
        squares = squares + ssq[j]
    inverse = lax.rsqrt(squares / (width * n_tp) + 1e-06)
    inverse = jnp.concatenate([inverse, jnp.zeros((128 - n_loc, FRAMES), F32)], axis=0).T
    for c in hop:
        c.wait()
    weights = []
    for a in range(tiles):
        inv = jnp.zeros((FRAMES, 128), F32)
        valid = jnp.zeros((FRAMES, 128), jnp.int32)
        for s in range(n_loc):
            inv = jnp.where(who[a] == s, inverse[:, s:s + 1], inv)
            valid = jnp.where(who[a] == s, fcnt[p * n_loc + s], valid)
        sc = sg[0, a * FRAMES:(a + 1) * FRAMES, :].astype(F32)
        for j in range(1, n_tp):
            sc = sc + sg[j, a * FRAMES:(a + 1) * FRAMES, :].astype(F32)
        sc = jnp.where(iota(sc.shape, 0) < valid, sc * (inv * scale), -1e30)
        top = jnp.max(sc, axis=0, keepdims=True)
        pr = jnp.exp(sc - top)
        norm = jnp.sum(pr, axis=0, keepdims=True)
        lse[p, a:a + 1, :] = top + jnp.log(norm)
        weights.append(pr * inv / norm)
    if tiles < lse.shape[1]:
        lse[p, tiles:, :] = jnp.zeros((lse.shape[1] - tiles, 128), F32)
    hop_l = to_pool(1, lambda peer: lse.at[p], lse.at[p])

    wide = jnp.concatenate(
        [jnp.concatenate([jnp.where(who[a] == s, weights[a], 0.0) for s in range(n_loc)], axis=0).T
         for a in range(tiles)], axis=0)
    ob = gather_heads(jnp.dot(wide.astype(BF), vp[...], preferred_element_type=F32)).astype(BF)
    sendo[...] = ob.reshape(n_pool, per * QH, HD)
    recvo[p] = sendo[p]
    hop = to_pool(2, lambda peer: sendo.at[peer], recvo.at[p])

    loads[2].wait()
    tops, sums = [], []

    def attend_cached(i):
        qb = spread_heads(qg[t, i * QH:(i + 1) * QH, :])
        rows = slice(i * SLOT_TOK, (i + 1) * SLOT_TOK)
        sc = lax.dot_general(qb, ca[rows, :HS], NT, preferred_element_type=F32) * scale
        sc = jnp.where(iota(sc.shape, 1) < lengths[i], sc, -1e30)
        top = jnp.max(sc, axis=1, keepdims=True)
        pr = jnp.exp(sc - top)
        tops.append(top)
        sums.append(jnp.sum(pr, axis=1, keepdims=True))
        oc[i * QH:(i + 1) * QH, :] = gather_heads(
            jnp.dot(pr.astype(BF), ca[rows, HS:], preferred_element_type=F32))

    for i in range(slots // 2):
        attend_cached(i)
    for c in hop_l:
        c.wait()
    fresh_lse = []
    offset = iota((QH, 128), 1) - iota((QH, 128), 0)
    for i in range(slots):
        spread = jnp.zeros((QH, 128), F32)
        for c in range(n_pool * per):
            u = p * per + c % per
            line = lse[c // per, pl.ds(u // PACK, 1), :]
            here = (offset == (u % PACK) * QH) & (mine[i] == c)
            spread = jnp.where(here, line, spread)
        fresh_lse.append(jnp.sum(spread, axis=1, keepdims=True))
    for c in hop:
        c.wait()

    moved = permute(held, recvo[...].reshape(n_loc * QH, HD))
    sendp[...] = moved.reshape(n_tp, slots * QH, HD)
    recvp[t] = sendp[t]
    hop = to_tp(3, lambda peer: sendp.at[peer], recvp.at[t])
    for i in range(slots // 2, slots):
        attend_cached(i)
    for c in hop:
        c.wait()
    for i in range(slots):
        rows = slice(i * QH, (i + 1) * QH)
        new = recvp[0, rows, :].astype(F32)
        for j in range(1, n_tp):
            new = new + recvp[j, rows, :].astype(F32)
        top = jnp.maximum(tops[i], fresh_lse[i])
        ea = jnp.exp(fresh_lse[i] - top)
        eb = jnp.exp(tops[i] - top)
        res = (ea * new + eb * oc[rows, :]) / (ea + eb * sums[i])
        out[rows, :] = jnp.where(mine[i] >= 0, res, 0.0).astype(BF)


def per_device(n_tp, n_pool, frames, norm_gain, kv_weight, kv_cache, queries, placement,
               cached_len, frame_count):
    rows, width = frames.shape
    slots = queries.shape[0]
    n_loc = rows // FRAMES
    per = n_loc // n_pool
    tiles = n_loc // PACK
    vm = pl.BlockSpec(memory_space=pltpu.VMEM)
    sm = pl.BlockSpec(memory_space=pltpu.SMEM)
    hbm = pl.BlockSpec(memory_space=pltpu.HBM)
    out = pl.pallas_call(
        functools.partial(kernel, n_tp, n_pool),
        out_shape=jax.ShapeDtypeStruct((slots * QH, HD), BF),
        in_specs=[sm, sm, sm, vm, vm, hbm, hbm, hbm],
        out_specs=vm,
        scratch_shapes=[
            pltpu.VMEM((rows, width), BF),
            pltpu.VMEM((width, HS), BF),
            pltpu.VMEM((width, HS), BF),
            pltpu.VMEM(kv_cache.shape, BF),
            pltpu.VMEM((rows, width), BF),
            pltpu.VMEM((rows, HS), BF),
            pltpu.VMEM((rows, HS), BF),
            pltpu.VMEM((n_tp, slots * QH, HD), BF),
            pltpu.VMEM((n_pool, per * QH, HD), BF),
            pltpu.VMEM((n_pool, per * QH, HD), BF),
            pltpu.VMEM((n_tp, n_loc, FRAMES), F32),
            pltpu.VMEM((n_tp, tiles * FRAMES, 128), BF),
            pltpu.VMEM((n_pool, max(8, tiles), 128), F32),
            pltpu.VMEM((n_pool, per * QH, HD), BF),
            pltpu.VMEM((n_pool, per * QH, HD), BF),
            pltpu.VMEM((n_tp, slots * QH, HD), BF),
            pltpu.VMEM((n_tp, slots * QH, HD), BF),
            pltpu.VMEM((slots * QH, HD), F32),
            pltpu.SemaphoreType.DMA((4,)),
            pltpu.SemaphoreType.DMA((4, n_tp)),
            pltpu.SemaphoreType.DMA((4, n_tp)),
            pltpu.SemaphoreType.DMA((3, n_pool)),
            pltpu.SemaphoreType.DMA((3, n_pool)),
        ],
        compiler_params=pltpu.CompilerParams(
            collective_id=0, has_side_effects=True, vmem_limit_bytes=62 * 1024 * 1024),
    )(placement, cached_len, frame_count, norm_gain,
      queries, frames, kv_weight, kv_cache)
    return out.reshape(slots, QH * HD)


def solution(mesh):
    return jax.shard_map(
        functools.partial(per_device, mesh.shape["tp"], mesh.shape["pool"]),
        mesh=mesh,
        in_specs=(
            P(("groups", "pool"), "tp"),
            P("tp"),
            P("tp", None),
            P(("groups", "tp", "pool"), None),
            P(("groups", "tp", "pool"), None),
            P("groups"),
            P("groups"),
            P("groups"),
        ),
        out_specs=P(("groups", "tp", "pool"), None),
        check_vma=False,
    )
```

```python
import functools

import jax
import jax.numpy as jnp
from jax import lax
from jax.experimental import pallas as pl
from jax.experimental.pallas import tpu as pltpu
from jax.sharding import PartitionSpec as P

QH = 32
KVH = 8
HD = 128
GRP = QH // KVH
HS = KVH * HD
FRAMES = 64
SLOT_TOK = 512
PACK = 128 // QH
F32 = jnp.float32
BF = jnp.bfloat16
NT = (((1,), (1,)), ((), ()))
TN = (((0,), (0,)), ((), ()))


def iota(shape, dim):
    return lax.broadcasted_iota(jnp.int32, shape, dim)


def spread_heads(rows):
    wide = jnp.concatenate([rows.astype(F32)] * KVH, axis=1)
    own = (iota(wide.shape, 0) % QH) // GRP == iota(wide.shape, 1) // HD
    return jnp.where(own, wide, 0.0).astype(BF)


def gather_heads(wide):
    head = (iota((wide.shape[0], HD), 0) % QH) // GRP
    out = jnp.zeros((wide.shape[0], HD), F32)
    for j in range(KVH):
        out = jnp.where(head == j, wide[:, j * HD:(j + 1) * HD], out)
    return out


def permute(picks, blocks):
    shape = (QH, blocks.shape[0])
    offset = iota(shape, 1) - iota(shape, 0)
    hot = jnp.concatenate([jnp.where(offset == pick * QH, 1.0, 0.0) for pick in picks], axis=0)
    return jnp.dot(hot.astype(BF), blocks, preferred_element_type=F32).astype(BF)


def kernel(n_tp, n_pool, place, clen, fcnt, gain, q, frames_h, w_h, cache_h, out,
           fr, wk, wv, ca, xs, kp, vp, qg, sendq, recvq, ssq, sg, lse, sendo, recvo,
           sendp, recvp, oc,
           ld, s_tp, r_tp, s_pl, r_pl):
    slots = q.shape[0]
    n_loc = fr.shape[0] // FRAMES
    per = n_loc // n_pool
    tiles = n_loc // PACK
    width = fr.shape[1]
    scale = HD ** -0.5
    t = lax.axis_index("tp")
    p = lax.axis_index("pool")

    loads = [
        pltpu.make_async_copy(frames_h, fr, ld.at[0]),
        pltpu.make_async_copy(w_h.at[:, pl.ds(0, HS)], wk, ld.at[1]),
        pltpu.make_async_copy(cache_h, ca, ld.at[2]),
        pltpu.make_async_copy(w_h.at[:, pl.ds(HS, HS)], wv, ld.at[3]),
    ]
    for c in loads:
        c.start()

    barrier = pltpu.get_barrier_semaphore()
    for d in range(1, n_tp):
        pl.semaphore_signal(barrier, inc=1, device_id={"tp": lax.rem(t + d, n_tp)},
                            device_id_type=pl.DeviceIdType.MESH)
    for d in range(1, n_pool):
        pl.semaphore_signal(barrier, inc=1, device_id={"pool": lax.rem(p + d, n_pool)},
                            device_id_type=pl.DeviceIdType.MESH)

    def to_tp(stage, src, dst):
        made = []
        for d in range(1, n_tp):
            peer = lax.rem(t + d, n_tp)
            made.append(pltpu.make_async_remote_copy(
                src_ref=src(peer), dst_ref=dst, send_sem=s_tp.at[stage, d],
                recv_sem=r_tp.at[stage, d], device_id={"tp": peer},
                device_id_type=pl.DeviceIdType.MESH))
        for c in made:
            c.start()
        return made

    def to_pool(stage, src, dst):
        made = []
        for d in range(1, n_pool):
            peer = lax.rem(p + d, n_pool)
            made.append(pltpu.make_async_remote_copy(
                src_ref=src(peer), dst_ref=dst, send_sem=s_pl.at[stage, d],
                recv_sem=r_pl.at[stage, d], device_id={"pool": peer},
                device_id_type=pl.DeviceIdType.MESH))
        for c in made:
            c.start()
        return made

    rows = [q[i:i + 1, h * HD:(h + 1) * HD].astype(F32) for i in range(slots) for h in range(QH)]
    qg[t] = jnp.concatenate(rows, axis=0).astype(BF)
    pl.semaphore_wait(barrier, n_tp - 1 + n_pool - 1)
    hop = to_tp(0, lambda peer: qg.at[t], qg.at[t])

    keys = []
    for g in range(n_pool):
        found = [jnp.int32(0)] * per
        count = jnp.int32(0)
        for s in range(g * n_loc, (g + 1) * n_loc):
            row = place[s]
            owner = row // slots
            match = owner % n_pool == p
            key = (owner // n_pool) * slots + row % slots
            for k in range(per):
                found[k] = jnp.where(match & (count == k), key, found[k])
            count = count + match.astype(jnp.int32)
        keys += found
    loads[0].wait()
    gain_row = gain[...].astype(F32).reshape(1, width)
    lane = iota((FRAMES, 128), 1)

    def scale_session(s, total):
        x = fr[s * FRAMES:(s + 1) * FRAMES, :].astype(F32)
        xs[s * FRAMES:(s + 1) * FRAMES, :] = (x * gain_row).astype(BF)
        return jnp.where(lane == s, jnp.sum(x * x, axis=1, keepdims=True), total)

    total = jnp.zeros((FRAMES, 128), F32)
    for s in range(n_loc):
        total = scale_session(s, total)

    ssq[t] = total.T[:n_loc]
    hop_sq = to_tp(1, lambda peer: ssq.at[t], ssq.at[t])
    for c in hop:
        c.wait()
    moved = permute(keys, qg[...].reshape(n_tp * slots * QH, HD))
    sendq[...] = moved.reshape(n_pool, per * QH, HD)
    recvq[p] = sendq[p]
    hop = to_pool(0, lambda peer: sendq.at[peer], recvq.at[p])

    held = []
    for o in range(n_tp * slots):
        which = jnp.int32(-1)
        for c in range(n_pool * per):
            which = jnp.where(keys[c] == o, c, which)
        held.append(which)
    counts = [jnp.int32(0)] * n_pool
    order = [jnp.int32(0)] * n_loc
    for s in range(n_loc):
        column = (place[p * n_loc + s] // slots) % n_pool
        for c in range(n_pool):
            match = column == c
            for k in range(per):
                u = c * per + k
                order[u] = jnp.where(match & (counts[c] == k), s, order[u])
            counts[c] = counts[c] + match.astype(jnp.int32)
    lengths, mine = [], []
    for i in range(slots):
        length = jnp.int32(0)
        for s in range(n_pool * n_loc):
            length = jnp.where(place[s] == (t * n_pool + p) * slots + i, clen[s], length)
        which = jnp.int32(-1)
        for c in range(n_pool * per):
            which = jnp.where(keys[c] == t * slots + i, c, which)
        lengths.append(length)
        mine.append(which)

    loads[1].wait()
    for s in range(0, n_loc, 2 * PACK):
        rows = slice(s * FRAMES, (s + 2 * PACK) * FRAMES)
        kp[rows, :] = jnp.dot(xs[rows, :], wk[...], preferred_element_type=F32).astype(BF)
    for c in hop:
        c.wait()

    who = []
    group = recvq[...].reshape(n_loc * QH, HD)
    for a in range(tiles):
        ids = jnp.zeros((FRAMES, 128), jnp.int32)
        for k in range(PACK):
            ids = jnp.where(lane // QH == k, order[a * PACK + k], ids)
        who.append(ids)
    full = lax.dot_general(kp[...], spread_heads(group), NT, preferred_element_type=F32)
    for a in range(tiles):
        packed = jnp.zeros((FRAMES, 128), F32)
        for s in range(n_loc):
            packed = jnp.where(who[a] == s, full[s * FRAMES:(s + 1) * FRAMES, a * 128:(a + 1) * 128],
                               packed)
        sg[t, a * FRAMES:(a + 1) * FRAMES, :] = packed.astype(BF)
    hop = to_tp(2, lambda peer: sg.at[t], sg.at[t])

    loads[3].wait()
    for s in range(0, n_loc, 2 * PACK):
        rows = slice(s * FRAMES, (s + 2 * PACK) * FRAMES)
        vp[rows, :] = jnp.dot(xs[rows, :], wv[...], preferred_element_type=F32).astype(BF)

    for c in hop_sq:
        c.wait()
    squares = ssq[0]
    for j in range(1, n_tp):
        squares = squares + ssq[j]
    inverse = lax.rsqrt(squares / (width * n_tp) + 1e-06)
    inverse = jnp.concatenate([inverse, jnp.zeros((128 - n_loc, FRAMES), F32)], axis=0).T
    for c in hop:
        c.wait()
    weights = []
    for a in range(tiles):
        inv = jnp.zeros((FRAMES, 128), F32)
        valid = jnp.zeros((FRAMES, 128), jnp.int32)
        for s in range(n_loc):
            inv = jnp.where(who[a] == s, inverse[:, s:s + 1], inv)
            valid = jnp.where(who[a] == s, fcnt[p * n_loc + s], valid)
        sc = sg[0, a * FRAMES:(a + 1) * FRAMES, :].astype(F32)
        for j in range(1, n_tp):
            sc = sc + sg[j, a * FRAMES:(a + 1) * FRAMES, :].astype(F32)
        sc = jnp.where(iota(sc.shape, 0) < valid, sc * (inv * scale), -1e30)
        top = jnp.max(sc, axis=0, keepdims=True)
        pr = jnp.exp(sc - top)
        norm = jnp.sum(pr, axis=0, keepdims=True)
        lse[p, a:a + 1, :] = top + jnp.log(norm)
        weights.append(pr * inv / norm)
    if tiles < lse.shape[1]:
        lse[p, tiles:, :] = jnp.zeros((lse.shape[1] - tiles, 128), F32)
    hop_l = to_pool(1, lambda peer: lse.at[p], lse.at[p])

    wide = jnp.concatenate(
        [jnp.concatenate([jnp.where(who[a] == s, weights[a], 0.0) for s in range(n_loc)], axis=0).T
         for a in range(tiles)], axis=0)
    ob = gather_heads(jnp.dot(wide.astype(BF), vp[...], preferred_element_type=F32)).astype(BF)
    sendo[...] = ob.reshape(n_pool, per * QH, HD)
    recvo[p] = sendo[p]
    hop = to_pool(2, lambda peer: sendo.at[peer], recvo.at[p])

    loads[2].wait()
    tops, sums = [], []

    def attend_cached(i):
        qb = spread_heads(qg[t, i * QH:(i + 1) * QH, :])
        rows = slice(i * SLOT_TOK, (i + 1) * SLOT_TOK)
        sc = lax.dot_general(qb, ca[rows, :HS], NT, preferred_element_type=F32) * scale
        sc = jnp.where(iota(sc.shape, 1) < lengths[i], sc, -1e30)
        top = jnp.max(sc, axis=1, keepdims=True)
        pr = jnp.exp(sc - top)
        tops.append(top)
        sums.append(jnp.sum(pr, axis=1, keepdims=True))
        oc[i * QH:(i + 1) * QH, :] = gather_heads(
            jnp.dot(pr.astype(BF), ca[rows, HS:], preferred_element_type=F32))

    for i in range(slots // 2):
        attend_cached(i)
    for c in hop_l:
        c.wait()
    fresh_lse = []
    offset = iota((QH, 128), 1) - iota((QH, 128), 0)
    for i in range(slots):
        spread = jnp.zeros((QH, 128), F32)
        for c in range(n_pool * per):
            u = p * per + c % per
            line = lse[c // per, pl.ds(u // PACK, 1), :]
            here = (offset == (u % PACK) * QH) & (mine[i] == c)
            spread = jnp.where(here, line, spread)
        fresh_lse.append(jnp.sum(spread, axis=1, keepdims=True))
    for c in hop:
        c.wait()

    moved = permute(held, recvo[...].reshape(n_loc * QH, HD))
    sendp[...] = moved.reshape(n_tp, slots * QH, HD)
    recvp[t] = sendp[t]
    hop = to_tp(3, lambda peer: sendp.at[peer], recvp.at[t])
    for i in range(slots // 2, slots):
        attend_cached(i)
    for c in hop:
        c.wait()
    for i in range(slots):
        rows = slice(i * QH, (i + 1) * QH)
        new = recvp[0, rows, :].astype(F32)
        for j in range(1, n_tp):
            new = new + recvp[j, rows, :].astype(F32)
        top = jnp.maximum(tops[i], fresh_lse[i])
        ea = jnp.exp(fresh_lse[i] - top)
        eb = jnp.exp(tops[i] - top)
        res = (ea * new + eb * oc[rows, :]) / (ea + eb * sums[i])
        out[rows, :] = jnp.where(mine[i] >= 0, res, 0.0).astype(BF)


def per_device(n_tp, n_pool, frames, norm_gain, kv_weight, kv_cache, queries, placement,
               cached_len, frame_count):
    rows, width = frames.shape
    slots = queries.shape[0]
    n_loc = rows // FRAMES
    per = n_loc // n_pool
    tiles = n_loc // PACK
    vm = pl.BlockSpec(memory_space=pltpu.VMEM)
    sm = pl.BlockSpec(memory_space=pltpu.SMEM)
    hbm = pl.BlockSpec(memory_space=pltpu.HBM)
    out = pl.pallas_call(
        functools.partial(kernel, n_tp, n_pool),
        out_shape=jax.ShapeDtypeStruct((slots * QH, HD), BF),
        in_specs=[sm, sm, sm, vm, vm, hbm, hbm, hbm],
        out_specs=vm,
        scratch_shapes=[
            pltpu.VMEM((rows, width), BF),
            pltpu.VMEM((width, HS), BF),
            pltpu.VMEM((width, HS), BF),
            pltpu.VMEM(kv_cache.shape, BF),
            pltpu.VMEM((rows, width), BF),
            pltpu.VMEM((rows, HS), BF),
            pltpu.VMEM((rows, HS), BF),
            pltpu.VMEM((n_tp, slots * QH, HD), BF),
            pltpu.VMEM((n_pool, per * QH, HD), BF),
            pltpu.VMEM((n_pool, per * QH, HD), BF),
            pltpu.VMEM((n_tp, n_loc, FRAMES), F32),
            pltpu.VMEM((n_tp, tiles * FRAMES, 128), BF),
            pltpu.VMEM((n_pool, max(8, tiles), 128), F32),
            pltpu.VMEM((n_pool, per * QH, HD), BF),
            pltpu.VMEM((n_pool, per * QH, HD), BF),
            pltpu.VMEM((n_tp, slots * QH, HD), BF),
            pltpu.VMEM((n_tp, slots * QH, HD), BF),
            pltpu.VMEM((slots * QH, HD), F32),
            pltpu.SemaphoreType.DMA((4,)),
            pltpu.SemaphoreType.DMA((4, n_tp)),
            pltpu.SemaphoreType.DMA((4, n_tp)),
            pltpu.SemaphoreType.DMA((3, n_pool)),
            pltpu.SemaphoreType.DMA((3, n_pool)),
        ],
        compiler_params=pltpu.CompilerParams(
            collective_id=0, has_side_effects=True, vmem_limit_bytes=62 * 1024 * 1024),
    )(placement, cached_len, frame_count, norm_gain,
      queries, frames, kv_weight, kv_cache)
    return out.reshape(slots, QH * HD)


def solution(mesh):
    return jax.shard_map(
        functools.partial(per_device, mesh.shape["tp"], mesh.shape["pool"]),
        mesh=mesh,
        in_specs=(
            P(("groups", "pool"), "tp"),
            P("tp"),
            P("tp", None),
            P(("groups", "tp", "pool"), None),
            P(("groups", "tp", "pool"), None),
            P("groups"),
            P("groups"),
            P("groups"),
        ),
        out_specs=P(("groups", "tp", "pool"), None),
        check_vma=False,
    )
```
